32 devices in a mesh: wide: 8 (over z, x), narrow: 4 (over y, core).
Axes of the slice: x: 2, y: 2, z: 4, core: 2. Of those that a mesh axis runs over, the one named last changes fastest.
Arguments:
- trial_x: float32 [65536, 128], P(('wide', 'narrow')), may hold values from -6 to 6
- trial_y: float32 [65536, 128], P(('wide', 'narrow')), may hold values from -6 to 6
- energy: float32 [65536], P(('wide', 'narrow')), may hold values from 1 to 4
- level_shift: float32 [128], replicated, may hold values from 0.1 to 0.5
- resonant_kernel: bfloat16 [256, 8, 256, 256], P(('wide', 'narrow')), may hold values from -0.0625 to 0.0625
- resonant_list: int32 [256, 8], P(('wide', 'narrow')), may hold values from 0 to 31, all different within a row
- coupling_kernel: bfloat16 [256, 8, 256, 256], P(('wide', 'narrow')), may hold values from -0.0625 to 0.0625
- coupling_list: int32 [256, 8], P(('wide', 'narrow')), may hold values from 0 to 31, all different within a row
- partner: int32 [8, 8192], P('wide'), may hold values from 0 to 8191, each once within a row
- exchange_basis: bfloat16 [65536, 1024], P(('wide', 'narrow')), may hold values from -0.046875 to 0.046875
Outputs:
- new_x: float32 [65536, 128], P(('wide', 'narrow'))
- new_y: float32 [65536, 128], P(('wide', 'narrow'))
The draws below stay inside these ranges and needn't reach their ends.
Inputs may be any that keep to these rules, and one draw needn't show every extreme that they name: `resonant_list`: each row lists 8 different column blocks. `coupling_list`: each row lists 8 different column blocks. `partner`: each row is a permutation of the patch rows.
All inputs are finite; a program needn't handle non-finite values.
Results may differ from the reference program's by a relative error of at most 0.0038.
Values may be sent and summed in bfloat16 or wider, within the bound.
A program may use at most 128 MiB of HBM per device.

```python
import jax
import jax.numpy as jnp
from jax import lax

NV = 128
BLK = 256
NBLK = 8
R = 1024
APPS = 2
PATCH = 8192
PAIRS = 65536
N_WIDE = 8


def shard_levels(rng, shape, cuts, smallest, top_value):
    def one(position, shards_of):
        draws = jax.random.uniform(jax.random.fold_in(jax.random.fold_in(rng, 6), position), (shards_of,), jnp.float32, smallest / len(cuts), top_value / len(cuts))
        return jnp.repeat(jnp.exp(draws), shape[position] // shards_of).reshape((-1,) + (1,) * (len(shape) - position - 1))

    level = one(*cuts[0])
    for cut in cuts[1:]:
        level = level * one(*cut)
    return level


def choose_distinct(own_key, rows, number_of, top, lift):
    ranking = jax.random.permutation(jax.random.fold_in(own_key, 1), number_of)
    boost = ranking
    for power in range(3):
        boost = boost * boost // number_of
    boost = boost * lift // number_of
    tickets = jax.random.randint(jax.random.fold_in(own_key, 2), (rows, number_of), 0, 4096) + boost
    sure = jax.random.permutation(jax.random.fold_in(own_key, 3), rows)[jnp.arange(number_of) % rows]
    tickets = jnp.where(jnp.arange(rows)[:, None] == sure[None, :], 1 << 14, tickets)
    merit = tickets * number_of + jnp.arange(number_of)
    return lax.top_k(merit.astype(jnp.int32), top)[1].astype(jnp.int32)


def scatter_about(own_key, shape, deviation, limit, pieces=(), held_as=jnp.bfloat16):
    array = deviation * jax.random.normal(own_key, shape, jnp.float32)
    if pieces:
        array = array * shard_levels(own_key, shape, pieces, -0.22, 0.18)
    return jnp.clip(array, -limit, limit).astype(held_as)


def setup_inputs(seed: int = 0) -> dict:
    arg_keys = jax.random.split(jax.random.key(seed), 11)
    return {
        "trial_x": scatter_about(arg_keys[0], (PAIRS, NV), 1.0, 6.0, ((0, 32),), jnp.float32),
        "trial_y": scatter_about(arg_keys[1], (PAIRS, NV), 1.0, 6.0, ((0, 32),), jnp.float32),
        "energy": jnp.clip(1.0 + 3.0 * jax.random.uniform(arg_keys[2], (PAIRS,), jnp.float32) ** shard_levels(arg_keys[2], (PAIRS,), ((0, 32),), -0.2, 0.2), 1.0, 4.0),
        "level_shift": jnp.clip(jax.random.uniform(arg_keys[3], (NV,), jnp.float32, 0.1, 0.5), 0.1, 0.5),
        "resonant_kernel": scatter_about(arg_keys[4], (PAIRS // BLK, NBLK, BLK, BLK), (NBLK * BLK * 4) ** -0.5, 0.0625, ((0, 32),)),
        "resonant_list": choose_distinct(arg_keys[5], (PAIRS // BLK), PATCH // BLK, NBLK, 0),
        "coupling_kernel": scatter_about(arg_keys[6], (PAIRS // BLK, NBLK, BLK, BLK), (NBLK * BLK * 4) ** -0.5, 0.0625, ((0, 32),)),
        "coupling_list": choose_distinct(arg_keys[7], (PAIRS // BLK), PATCH // BLK, NBLK, 0),
        "partner": jax.vmap(lambda own: jax.random.permutation(own, PATCH))(jax.random.split(arg_keys[8], N_WIDE)).reshape((N_WIDE, PATCH)).astype(jnp.int32),
        "exchange_basis": scatter_about(arg_keys[9], (PAIRS, R), (PAIRS // 4) ** -0.5, 0.046875, ((0, 32),)),
    }


def patch_products(operands):
    own_patch, mirror_patch, res_kernel, res_list, cp_kernel, cp_list, perm_row = operands
    columns = own_patch.shape[1]
    offsets = jnp.arange(BLK, dtype=jnp.int32)
    own_tiles = own_patch[(res_list[:, :, None] * BLK + offsets).astype(jnp.int32)].astype(jnp.float32)
    mirror_tiles = mirror_patch[perm_row.reshape(-1, BLK)[cp_list]].astype(jnp.float32)
    resonant = jnp.einsum("bnij,bnjc->bic", res_kernel.astype(jnp.float32), own_tiles)
    coupling = jnp.einsum("bnij,bnjc->bic", cp_kernel.astype(jnp.float32), mirror_tiles)
    return resonant.reshape(-1, columns), coupling.reshape(-1, columns)


def apply_once(trial_x, trial_y, energy, level_shift, resonant_kernel, resonant_list, coupling_kernel, coupling_list, partner, exchange_basis):
    vectors = trial_x.shape[1]
    columns = 2 * vectors
    stacked = jnp.concatenate([trial_x.astype(jnp.bfloat16), trial_y.astype(jnp.bfloat16)], axis=1)
    patches = stacked.reshape(N_WIDE, PATCH, columns)
    mirrored = jnp.roll(patches, N_WIDE // 2, axis=0)
    blocks = PATCH // BLK
    res_kernel = resonant_kernel.reshape(N_WIDE, blocks, NBLK, BLK, BLK)
    res_list = resonant_list.reshape(N_WIDE, blocks, NBLK)
    cp_kernel = coupling_kernel.reshape(N_WIDE, blocks, NBLK, BLK, BLK)
    cp_list = coupling_list.reshape(N_WIDE, blocks, NBLK)
    resonant, coupling = lax.map(patch_products, (patches, mirrored, res_kernel, res_list, cp_kernel, cp_list, partner))
    resonant = resonant.reshape(-1, columns)
    coupling = coupling.reshape(-1, columns)
    summed = (trial_x + trial_y).astype(jnp.bfloat16)
    weights = lax.dot_general(exchange_basis, summed, (((0,), (0,)), ((), ())), preferred_element_type=jnp.float32)
    exchange = jnp.dot(exchange_basis, weights.astype(jnp.bfloat16), preferred_element_type=jnp.float32)
    levels = energy[:, None]
    shifts = level_shift[None, :]
    image_x = levels * trial_x + resonant[:, :vectors] + coupling[:, vectors:] + exchange
    image_y = -(levels * trial_y + resonant[:, vectors:] + coupling[:, :vectors] + exchange)
    next_x = (image_x - shifts * trial_x) / (levels - shifts)
    next_y = -(image_y - shifts * trial_y) / (levels + shifts)
    return next_x, next_y


def reference(trial_x, trial_y, energy, level_shift, resonant_kernel, resonant_list, coupling_kernel, coupling_list, partner, exchange_basis):
    current_x, current_y = trial_x, trial_y
    for app_index in range(APPS):
        current_x, current_y = apply_once(current_x, current_y, energy, level_shift, resonant_kernel, resonant_list, coupling_kernel, coupling_list, partner, exchange_basis)
    return current_x, current_y
```

```python
import functools

import jax
import jax.numpy as jnp
from jax import lax
from jax.experimental import pallas as pl
from jax.experimental.pallas import tpu as pltpu
from jax.sharding import PartitionSpec as P

BLK = 256
APPS = 2
CH = 2
PIECES = 4
MESH = pl.DeviceIdType.MESH
F32 = jnp.float32
BF16 = jnp.bfloat16


def kernel(nw, nn, x_ref, y_ref, e_ref, s_ref, rl_ref, cl_ref, pr_ref, rk_ref, ck_ref, ub_ref,
           ox_ref, oy_ref,
           rkv, ckv, ubv, own0, own1, own2, own3, mir, stage, tile, perm, state, kres, wpart, wrs, wsnd, wrcv, wsum, wfull,
           ld_sem, z_s, z_r, py_s, py_r, ps_s, ps_r, pf_s, pf_r, my_s, my_r, ms_s, ms_r, mf_s, mf_r,
           rs_s, rs_r, wd_s, wd_r, ag_s, ag_r):
    owns = (own0, own1, own2, own3)
    w = lax.axis_index("wide")
    n = lax.axis_index("narrow")
    bits = nw.bit_length() - 1
    sib = n + 1 - 2 * lax.rem(n, 2)
    yp = lax.rem(n + 2, nn)
    ysib = lax.rem(sib + 2, nn)
    wpeers = [w + (1 << b) * (1 - 2 * lax.rem(w // (1 << b), 2)) for b in range(bits)]
    mirror = wpeers[bits - 1]

    rows = x_ref.shape[0]
    half = x_ref.shape[1] // 2
    blocks = rows // BLK
    nblk = rkv.shape[0] // blocks
    patch = rows * nn
    rank_share = ubv.shape[1] // nn

    loads = [
        pltpu.make_async_copy(ub_ref, ubv, ld_sem.at[0]),
        pltpu.make_async_copy(rk_ref, rkv, ld_sem.at[1]),
        pltpu.make_async_copy(ck_ref, ckv, ld_sem.at[2]),
    ]
    for load in loads:
        load.start()

    barrier = pltpu.get_barrier_semaphore()
    peers = [(w, lax.rem(n + j, nn)) for j in range(1, nn)] + [(p, n) for p in wpeers]
    for peer in peers:
        pl.semaphore_signal(barrier, inc=1, device_id=peer, device_id_type=MESH)

    low = lax.broadcasted_iota(jnp.int32, (BLK, 2 * half), 1) < half
    shift_row = jnp.broadcast_to(s_ref[...], (8, 2 * half))
    low8 = lax.broadcasted_iota(jnp.int32, (8, 2 * half), 1) < half
    turned = pltpu.roll(shift_row, half, 1)
    signed = [
        jnp.where(low8, -shift_row, turned)[0:1],
        jnp.where(low8, -turned, shift_row)[0:1],
    ]

    pending = []

    def send(src, dst, ssem, rsem, device):
        copy = pltpu.make_async_remote_copy(
            src_ref=src, dst_ref=dst, send_sem=ssem, recv_sem=rsem, device_id=device, device_id_type=MESH
        )
        copy.start()
        pending.append(copy)

    def arrived(ref, ssem, rsem, device):
        pltpu.make_async_remote_copy(
            src_ref=ref, dst_ref=ref, send_sem=ssem, recv_sem=rsem, device_id=device, device_id_type=MESH
        ).wait_recv()

    def part(buf, t, who, p):
        return buf.at[t, pl.ds(who * blocks + p * (blocks // PIECES), blocks // PIECES)]

    def held(t, who, p):
        return owns[t].at[pl.ds(who * blocks + p * (blocks // PIECES), blocks // PIECES)]

    def send_z(t, p):
        send(held(t, n, p), part(mir, t, n, p), z_s.at[t, p], z_r.at[t, p], (mirror, n))

    def send_own(t, p):
        send(held(t, n, p), held(t, n, p), py_s.at[t, p], py_r.at[t, p], (w, yp))
        send(held(t, n, p), held(t, n, p), ps_s.at[t, p], ps_r.at[t, p], (w, sib))

    def forward_own(t, p):
        arrived(held(t, yp, p), py_s.at[t, p], py_r.at[t, p], (w, yp))
        send(held(t, yp, p), held(t, yp, p), pf_s.at[t, p], pf_r.at[t, p], (w, sib))

    def finish_own(t):
        for p in range(PIECES):
            arrived(held(t, sib, p), ps_s.at[t, p], ps_r.at[t, p], (w, sib))
            arrived(held(t, ysib, p), pf_s.at[t, p], pf_r.at[t, p], (w, sib))

    def relay_z(t, p):
        arrived(part(mir, t, n, p), z_s.at[t, p], z_r.at[t, p], (mirror, n))
        send(part(mir, t, n, p), part(mir, t, n, p), my_s.at[t, p], my_r.at[t, p], (w, yp))
        send(part(mir, t, n, p), part(mir, t, n, p), ms_s.at[t, p], ms_r.at[t, p], (w, sib))

    def forward_mir(t, p):
        arrived(part(mir, t, yp, p), my_s.at[t, p], my_r.at[t, p], (w, yp))
        send(part(mir, t, yp, p), part(mir, t, yp, p), mf_s.at[t, p], mf_r.at[t, p], (w, sib))

    def finish_mir(t):
        for p in range(PIECES):
            arrived(part(mir, t, sib, p), ms_s.at[t, p], ms_r.at[t, p], (w, sib))
            arrived(part(mir, t, ysib, p), mf_s.at[t, p], mf_r.at[t, p], (w, sib))

    def project(t, c):
        z = state[c]
        summed = (z + pltpu.roll(z, half, 1)).astype(BF16)
        flipped = summed.T[:half]
        for q in range(nn):
            share = jnp.dot(flipped, ubv[:, q * rank_share:(q + 1) * rank_share], preferred_element_type=F32)
            wpart[t, q] = share.astype(BF16)

        for j in range(1, nn):
            to = lax.rem(n + j, nn)
            send(wpart.at[t, to], wrs.at[t, j - 1], rs_s.at[t, j - 1], rs_r.at[t, j - 1], (w, to))

    def wide_send(t, b):
        wsnd[t, b] = wsum[t].astype(BF16)
        send(wsnd.at[t, b], wrcv.at[t, b], wd_s.at[t, b], wd_r.at[t, b], (wpeers[b], n))

    def sum_narrow(t):
        total = wpart[t, n].astype(F32)
        for j in range(1, nn):
            arrived(wrs.at[t, j - 1], rs_s.at[t, j - 1], rs_r.at[t, j - 1], (w, lax.rem(n + j, nn)))
            total = total + wrs[t, j - 1].astype(F32)
        wsum[t] = total
        wide_send(t, 0)

    def sum_wide(t, b):
        arrived(wrcv.at[t, b], wd_s.at[t, b], wd_r.at[t, b], (wpeers[b], n))
        wsum[t] = wsum[t] + wrcv[t, b].astype(F32)
        if b + 1 < bits:
            wide_send(t, b + 1)
            return
        wfull[t, n] = wsum[t].astype(BF16)
        for j in range(1, nn):
            to = lax.rem(n + j, nn)
            send(wfull.at[t, n], wfull.at[t, n], ag_s.at[t, j - 1], ag_r.at[t, j - 1], (w, to))

    def finish_exchange(t):
        for j in range(1, nn):
            come = lax.rem(n - j + nn, nn)
            arrived(wfull.at[t, come], ag_s.at[t, j - 1], ag_r.at[t, j - 1], (w, lax.rem(n + j, nn)))

    def set_up(c):
        def body(i, _):
            at = pl.ds(pl.multiple_of(i * BLK, BLK), BLK)
            x, y = x_ref[at, :], y_ref[at, :]
            if c == 0:
                z = jnp.where(low, x, pltpu.roll(y, half, 1))
            else:
                z = jnp.where(low, pltpu.roll(x, half, 1), y)
            state[c, at, :] = z
            owns[c][n * blocks + i] = z.astype(BF16)
            return 0

        lax.fori_loop(0, blocks, body, 0)

    def block_sum(kernels, lists, source, b):
        total = jnp.zeros((BLK, 2 * half), F32)
        for k in range(nblk):
            total = total + jnp.dot(
                kernels[b * nblk + k], source[lists[b * nblk + k]], preferred_element_type=F32
            )
        return total

    def resonant(t, c):
        def body(b, _):
            kres[c, pl.ds(pl.multiple_of(b * BLK, BLK), BLK), :] = block_sum(
                rkv, rl_ref, owns[t], b
            )
            return 0

        lax.fori_loop(0, blocks, body, 0)

    def widen(t):
        def body(i, _):
            at = pl.ds(pl.multiple_of(i * BLK, BLK), BLK)
            stage[at, :] = mir[t, i].astype(F32)
            return 0

        lax.fori_loop(0, patch // BLK, body, 0)

    def permute(first, last):
        step = 64
        per = BLK // step

        def body(i, _):
            for g in range(per):
                base = i * BLK + g * step
                for j in range(step):
                    tile[j] = stage[pr_ref[base + j]]
                perm[i, g * step:(g + 1) * step, :] = tile[...].astype(BF16)
            return 0

        lax.fori_loop(first * patch // BLK // 4, last * patch // BLK // 4, body, 0)

    def update(a, c, first, last):
        t = a * CH + c
        sign = signed[c]

        def body(b, _):
            at = pl.ds(pl.multiple_of(b * BLK, BLK), BLK)
            kc = block_sum(ckv, cl_ref, perm, b)
            total = kres[c, at, :] + pltpu.roll(kc, half, 1)
            for q in range(nn):
                share = wfull[t, q]
                total = total + lax.dot_general(
                    ubv[at, q * rank_share:(q + 1) * rank_share],
                    jnp.concatenate([share, share], axis=0),
                    (((1,), (1,)), ((), ())),
                    preferred_element_type=F32,
                )
            level = e_ref[at, :]
            z = state[c, at, :]
            new = (level * z + total + sign * z) / (level + sign)
            if a + 1 < APPS:
                state[c, at, :] = new
                owns[t + CH][n * blocks + b] = new.astype(BF16)
            elif c == 0:
                state[c, at, :] = new
            else:
                z0 = state[0, at, :]
                ox_ref[at, :] = jnp.where(low, z0, pltpu.roll(new, half, 1))
                oy_ref[at, :] = jnp.where(low, pltpu.roll(z0, half, 1), new)
            return 0

        lax.fori_loop(first, last, body, 0)

    set_up(0)
    pl.semaphore_wait(barrier, len(peers))
    for p in range(PIECES):
        send_z(0, p)
        send_own(0, p)
    set_up(1)
    loads[0].wait()
    project(0, 0)
    project(1, 1)
    relay_z(0, 0)
    sum_narrow(0)
    sum_narrow(1)
    send_z(1, 0)
    for p in range(PIECES):
        forward_own(0, p)
        if p % 2 == 0:
            send_own(1, p)
    forward_mir(0, 0)
    for b in range(bits):
        sum_wide(0, b)
        sum_wide(1, b)
        if b == 0:
            relay_z(0, 1)
            send_z(1, 1)
    finish_own(0)
    loads[1].wait()
    resonant(0, 0)
    forward_mir(0, 1)
    relay_z(0, 2)
    send_z(1, 2)
    send_own(1, 1)
    send_own(1, 3)
    forward_mir(0, 2)
    relay_z(0, 3)
    send_z(1, 3)
    finish_exchange(0)
    finish_exchange(1)
    forward_mir(0, 3)
    loads[2].wait()

    quarter = blocks // 2
    total_t = APPS * CH
    for a in range(APPS):
        for c in range(CH):
            t = a * CH + c
            finish_mir(t)
            widen(t)
            later = t + 1 if t + 1 < total_t else None
            permute(0, 2)
            if later is not None:
                relay_z(later, 0)
            permute(2, 4)
            if later is not None:
                forward_mir(later, 0)
            update(a, c, 0, quarter)
            if a + 1 < APPS:
                for p in range(PIECES // 2):
                    send_z(t + CH, p)
            if later is not None:
                relay_z(later, 1)
            update(a, c, quarter, blocks)
            if a + 1 < APPS:
                for p in range(PIECES // 2, PIECES):
                    send_z(t + CH, p)
                for p in range(PIECES):
                    send_own(t + CH, p)
                project(t + CH, c)
            if later is None:
                continue
            forward_mir(later, 1)
            for p in range(PIECES):
                forward_own(later, p)
            finish_own(later)
            if a + 1 < APPS:
                sum_narrow(t + CH)
            resonant(later, later % CH)
            relay_z(later, 2)
            forward_mir(later, 2)
            if a + 1 < APPS:
                for b in range(bits):
                    sum_wide(t + CH, b)
            relay_z(later, 3)
            forward_mir(later, 3)
            if a + 1 < APPS:
                finish_exchange(t + CH)
    for copy in pending:
        copy.wait_send()


def on_device(nw, nn, trial_x, trial_y, energy, level_shift, resonant_kernel, resonant_list,
              coupling_kernel, coupling_list, partner, exchange_basis):
    rows, vectors = trial_x.shape
    rank = exchange_basis.shape[1]
    blocks, nblk = resonant_list.shape
    patch = rows * nn
    slots = APPS * CH
    bits = nw.bit_length() - 1
    half = vectors // 2
    share = rank // nn
    vmem = pl.BlockSpec(memory_space=pltpu.VMEM)
    smem = pl.BlockSpec(memory_space=pltpu.SMEM)
    anywhere = pl.BlockSpec(memory_space=pl.ANY)
    dma = pltpu.SemaphoreType.DMA
    pieces = [dma((slots, PIECES))] * 14
    flat = (blocks * nblk, BLK, BLK)
    new_x, new_y = pl.pallas_call(
        functools.partial(kernel, nw, nn),
        out_shape=[jax.ShapeDtypeStruct((rows, vectors), F32)] * 2,
        in_specs=[vmem] * 4 + [smem] * 3 + [anywhere] * 3,
        out_specs=[vmem] * 2,
        scratch_shapes=[
            pltpu.VMEM(flat, BF16),
            pltpu.VMEM(flat, BF16),
            pltpu.VMEM((rows, rank), BF16),
            *[pltpu.VMEM((patch // BLK, BLK, vectors), BF16)] * slots,
            pltpu.VMEM((slots, patch // BLK, BLK, vectors), BF16),
            pltpu.VMEM((patch, vectors), F32),
            pltpu.VMEM((64, vectors), F32),
            pltpu.VMEM((patch // BLK, BLK, vectors), BF16),
            pltpu.VMEM((CH, rows, vectors), F32),
            pltpu.VMEM((CH, rows, vectors), F32),
            pltpu.VMEM((slots, nn, half, share), BF16),
            pltpu.VMEM((slots, nn - 1, half, share), BF16),
            pltpu.VMEM((slots, bits, half, share), BF16),
            pltpu.VMEM((slots, bits, half, share), BF16),
            pltpu.VMEM((slots, half, share), F32),
            pltpu.VMEM((slots, nn, half, share), BF16),
            dma((3,)),
            *pieces,
            dma((slots, nn - 1)),
            dma((slots, nn - 1)),
            dma((slots, bits)),
            dma((slots, bits)),
            dma((slots, nn - 1)),
            dma((slots, nn - 1)),
        ],
        compiler_params=pltpu.CompilerParams(
            collective_id=0, has_side_effects=True, vmem_limit_bytes=63 * 1024 * 1024
        ),
    )(
        trial_x,
        trial_y,
        energy[:, None],
        level_shift[None, :],
        resonant_list.reshape(-1),
        coupling_list.reshape(-1),
        partner.reshape(-1),
        resonant_kernel.reshape(flat),
        coupling_kernel.reshape(flat),
        exchange_basis,
    )
    return new_x, new_y


def solution(mesh):
    nw, nn = mesh.shape["wide"], mesh.shape["narrow"]
    rows = P(("wide", "narrow"), None)
    return jax.shard_map(
        functools.partial(on_device, nw, nn),
        mesh=mesh,
        in_specs=(
            rows,
            rows,
            P(("wide", "narrow")),
            P(),
            P(("wide", "narrow"), None, None, None),
            rows,
            P(("wide", "narrow"), None, None, None),
            rows,
            P("wide", None),
            rows,
        ),
        out_specs=(rows, rows),
        check_vma=False,
    )
```

```python
import functools

import jax
import jax.numpy as jnp
from jax import lax
from jax.experimental import pallas as pl
from jax.experimental.pallas import tpu as pltpu
from jax.sharding import PartitionSpec as P

BLK = 256
APPS = 2
CH = 2
PIECES = 4
MESH = pl.DeviceIdType.MESH
F32 = jnp.float32
BF16 = jnp.bfloat16


def kernel(nw, nn, x_ref, y_ref, e_ref, s_ref, rl_ref, cl_ref, pr_ref, rk_ref, ck_ref, ub_ref,
           ox_ref, oy_ref,
           rkv, ckv, ubv, own0, own1, own2, own3, mir, stage, tile, perm, state, kres, wpart, wrs, wsnd, wrcv, wsum, wfull,
           ld_sem, z_s, z_r, py_s, py_r, ps_s, ps_r, pf_s, pf_r, my_s, my_r, ms_s, ms_r, mf_s, mf_r,
           rs_s, rs_r, wd_s, wd_r, ag_s, ag_r):
    owns = (own0, own1, own2, own3)
    w = lax.axis_index("wide")
    n = lax.axis_index("narrow")
    bits = nw.bit_length() - 1
    sib = n + 1 - 2 * lax.rem(n, 2)
    yp = lax.rem(n + 2, nn)
    ysib = lax.rem(sib + 2, nn)
    wpeers = [w + (1 << b) * (1 - 2 * lax.rem(w // (1 << b), 2)) for b in range(bits)]
    mirror = wpeers[bits - 1]
    wpeers = wpeers[::-1]

    rows = x_ref.shape[0]
    half = x_ref.shape[1] // 2
    blocks = rows // BLK
    nblk = rkv.shape[0] // blocks
    patch = rows * nn
    rank_share = ubv.shape[1] // nn

    loads = [
        pltpu.make_async_copy(ub_ref, ubv, ld_sem.at[0]),
        pltpu.make_async_copy(rk_ref, rkv, ld_sem.at[1]),
        pltpu.make_async_copy(ck_ref, ckv, ld_sem.at[2]),
    ]
    for load in loads:
        load.start()

    barrier = pltpu.get_barrier_semaphore()
    peers = [(w, lax.rem(n + j, nn)) for j in range(1, nn)] + [(p, n) for p in wpeers]
    for peer in peers:
        pl.semaphore_signal(barrier, inc=1, device_id=peer, device_id_type=MESH)

    low = lax.broadcasted_iota(jnp.int32, (BLK, 2 * half), 1) < half
    shift_row = jnp.broadcast_to(s_ref[...], (8, 2 * half))
    low8 = lax.broadcasted_iota(jnp.int32, (8, 2 * half), 1) < half
    turned = pltpu.roll(shift_row, half, 1)
    signed = [
        jnp.where(low8, -shift_row, turned)[0:1],
        jnp.where(low8, -turned, shift_row)[0:1],
    ]

    pending = []

    def send(src, dst, ssem, rsem, device):
        copy = pltpu.make_async_remote_copy(
            src_ref=src, dst_ref=dst, send_sem=ssem, recv_sem=rsem, device_id=device, device_id_type=MESH
        )
        copy.start()
        pending.append(copy)

    def arrived(ref, ssem, rsem, device):
        pltpu.make_async_remote_copy(
            src_ref=ref, dst_ref=ref, send_sem=ssem, recv_sem=rsem, device_id=device, device_id_type=MESH
        ).wait_recv()

    def part(buf, t, who, p):
        return buf.at[t, pl.ds(who * blocks + p * (blocks // PIECES), blocks // PIECES)]

    def held(t, who, p):
        return owns[t].at[pl.ds(who * blocks + p * (blocks // PIECES), blocks // PIECES)]

    def send_z(t, p):
        send(held(t, n, p), part(mir, t, n, p), z_s.at[t, p], z_r.at[t, p], (mirror, n))

    def send_own(t, p):
        send(held(t, n, p), held(t, n, p), py_s.at[t, p], py_r.at[t, p], (w, yp))
        send(held(t, n, p), held(t, n, p), ps_s.at[t, p], ps_r.at[t, p], (w, sib))

    def forward_own(t, p):
        arrived(held(t, yp, p), py_s.at[t, p], py_r.at[t, p], (w, yp))
        send(held(t, yp, p), held(t, yp, p), pf_s.at[t, p], pf_r.at[t, p], (w, sib))

    def finish_own(t):
        for p in range(PIECES):
            arrived(held(t, sib, p), ps_s.at[t, p], ps_r.at[t, p], (w, sib))
            arrived(held(t, ysib, p), pf_s.at[t, p], pf_r.at[t, p], (w, sib))

    def relay_z(t, p):
        arrived(part(mir, t, n, p), z_s.at[t, p], z_r.at[t, p], (mirror, n))
        send(part(mir, t, n, p), part(mir, t, n, p), my_s.at[t, p], my_r.at[t, p], (w, yp))
        send(part(mir, t, n, p), part(mir, t, n, p), ms_s.at[t, p], ms_r.at[t, p], (w, sib))

    def forward_mir(t, p):
        arrived(part(mir, t, yp, p), my_s.at[t, p], my_r.at[t, p], (w, yp))
        send(part(mir, t, yp, p), part(mir, t, yp, p), mf_s.at[t, p], mf_r.at[t, p], (w, sib))

    def finish_mir(t):
        for p in range(PIECES):
            arrived(part(mir, t, sib, p), ms_s.at[t, p], ms_r.at[t, p], (w, sib))
            arrived(part(mir, t, ysib, p), mf_s.at[t, p], mf_r.at[t, p], (w, sib))

    def project(t, c):
        z = state[c]
        summed = (z + pltpu.roll(z, half, 1)).astype(BF16)
        flipped = summed.T[:half]
        for q in range(nn):
            share = jnp.dot(flipped, ubv[:, q * rank_share:(q + 1) * rank_share], preferred_element_type=F32)
            wpart[t, q] = share

        for j in range(1, nn):
            to = lax.rem(n + j, nn)
            send(wpart.at[t, to], wrs.at[t, j - 1], rs_s.at[t, j - 1], rs_r.at[t, j - 1], (w, to))

    def wide_send(t, b):
        wsnd[t, b] = wsum[t]
        send(wsnd.at[t, b], wrcv.at[t, b], wd_s.at[t, b], wd_r.at[t, b], (wpeers[b], n))

    def sum_narrow(t):
        total = wpart[t, n]
        for j in range(1, nn):
            arrived(wrs.at[t, j - 1], rs_s.at[t, j - 1], rs_r.at[t, j - 1], (w, lax.rem(n + j, nn)))
            total = total + wrs[t, j - 1]
        wsum[t] = total
        wide_send(t, 0)

    def sum_wide(t, b):
        arrived(wrcv.at[t, b], wd_s.at[t, b], wd_r.at[t, b], (wpeers[b], n))
        wsum[t] = wsum[t] + wrcv[t, b]
        if b + 1 < bits:
            wide_send(t, b + 1)
            return
        wfull[t, n] = wsum[t].astype(BF16)
        for j in range(1, nn):
            to = lax.rem(n + j, nn)
            send(wfull.at[t, n], wfull.at[t, n], ag_s.at[t, j - 1], ag_r.at[t, j - 1], (w, to))

    def finish_exchange(t):
        for j in range(1, nn):
            come = lax.rem(n - j + nn, nn)
            arrived(wfull.at[t, come], ag_s.at[t, j - 1], ag_r.at[t, j - 1], (w, lax.rem(n + j, nn)))

    def set_up(c):
        def body(i, _):
            at = pl.ds(pl.multiple_of(i * BLK, BLK), BLK)
            x, y = x_ref[at, :], y_ref[at, :]
            if c == 0:
                z = jnp.where(low, x, pltpu.roll(y, half, 1))
            else:
                z = jnp.where(low, pltpu.roll(x, half, 1), y)
            state[c, at, :] = z
            owns[c][n * blocks + i] = z.astype(BF16)
            return 0

        lax.fori_loop(0, blocks, body, 0)

    def block_sum(kernels, lists, source, b):
        total = jnp.zeros((BLK, 2 * half), F32)
        for k in range(nblk):
            total = total + jnp.dot(
                kernels[b * nblk + k], source[lists[b * nblk + k]], preferred_element_type=F32
            )
        return total

    def resonant(t, c):
        def body(b, _):
            kres[c, pl.ds(pl.multiple_of(b * BLK, BLK), BLK), :] = block_sum(
                rkv, rl_ref, owns[t], b
            )
            return 0

        lax.fori_loop(0, blocks, body, 0)

    def widen(t):
        def body(i, _):
            at = pl.ds(pl.multiple_of(i * BLK, BLK), BLK)
            stage[at, :] = mir[t, i].astype(F32)
            return 0

        lax.fori_loop(0, patch // BLK, body, 0)

    def permute(first, last):
        step = 64
        per = BLK // step

        def body(i, _):
            for g in range(per):
                base = i * BLK + g * step
                for j in range(step):
                    tile[j] = stage[pr_ref[base + j]]
                perm[i, g * step:(g + 1) * step, :] = tile[...].astype(BF16)
            return 0

        lax.fori_loop(first * patch // BLK // 4, last * patch // BLK // 4, body, 0)

    def update(a, c, first, last):
        t = a * CH + c
        sign = signed[c]

        def body(b, _):
            at = pl.ds(pl.multiple_of(b * BLK, BLK), BLK)
            kc = block_sum(ckv, cl_ref, perm, b)
            total = kres[c, at, :] + pltpu.roll(kc, half, 1)
            for q in range(nn):
                share = wfull[t, q]
                total = total + lax.dot_general(
                    ubv[at, q * rank_share:(q + 1) * rank_share],
                    jnp.concatenate([share, share], axis=0),
                    (((1,), (1,)), ((), ())),
                    preferred_element_type=F32,
                )
            level = e_ref[at, :]
            z = state[c, at, :]
            new = (level * z + total + sign * z) / (level + sign)
            if a + 1 < APPS:
                state[c, at, :] = new
                owns[t + CH][n * blocks + b] = new.astype(BF16)
            elif c == 0:
                state[c, at, :] = new
            else:
                z0 = state[0, at, :]
                ox_ref[at, :] = jnp.where(low, z0, pltpu.roll(new, half, 1))
                oy_ref[at, :] = jnp.where(low, pltpu.roll(z0, half, 1), new)
            return 0

        lax.fori_loop(first, last, body, 0)

    set_up(0)
    pl.semaphore_wait(barrier, len(peers))
    send_z(0, 0)
    send_z(0, 1)
    send_own(0, 0)
    set_up(1)
    loads[0].wait()
    project(0, 0)
    project(1, 1)
    for p in range(1, PIECES):
        send_own(0, p)
    relay_z(0, 0)
    send_z(0, 2)
    sum_narrow(0)
    sum_narrow(1)
    send_z(0, 3)
    forward_own(0, 0)
    forward_mir(0, 0)
    relay_z(0, 1)
    send_z(1, 0)
    for p in range(1, PIECES):
        forward_own(0, p)
    finish_own(0)
    loads[1].wait()
    resonant(0, 0)
    relay_z(0, 2)
    send_z(1, 1)
    send_own(1, 0)
    forward_mir(0, 1)
    sum_wide(0, 0)
    sum_wide(1, 0)
    forward_mir(0, 2)
    send_own(1, 1)
    relay_z(0, 3)
    send_z(1, 2)
    for b in range(1, bits - 1):
        sum_wide(0, b)
        sum_wide(1, b)
    forward_mir(0, 3)
    send_z(1, 3)
    send_own(1, 2)
    send_own(1, 3)
    sum_wide(0, bits - 1)
    sum_wide(1, bits - 1)
    loads[2].wait()

    middle = blocks // 2
    total_t = APPS * CH
    for a in range(APPS):
        for c in range(CH):
            t = a * CH + c
            later = t + 1 if t + 1 < total_t else None
            more = a + 1 < APPS
            finish_mir(t)
            widen(t)
            permute(0, 1)
            if a > 0:
                for b in range(1, bits - 1):
                    sum_wide(t, b)
            permute(1, 2)
            if later is not None:
                relay_z(later, 0)
            permute(2, 3)
            if a > 0:
                sum_wide(t, bits - 1)
            permute(3, 4)
            if later is not None:
                forward_mir(later, 0)
            finish_exchange(t)
            update(a, c, 0, middle)
            if more:
                for p in range(PIECES // 2):
                    send_z(t + CH, p)
            if later is not None:
                relay_z(later, 1)
            update(a, c, middle, blocks)
            if more:
                for p in range(PIECES // 2, PIECES):
                    send_z(t + CH, p)
                project(t + CH, c)
            if later is None:
                continue
            forward_mir(later, 1)
            for p in range(PIECES):
                forward_own(later, p)
            finish_own(later)
            resonant(later, later % CH)
            relay_z(later, 2)
            forward_mir(later, 2)
            if more:
                sum_narrow(t + CH)
            relay_z(later, 3)
            if more:
                for p in range(PIECES):
                    send_own(t + CH, p)
            forward_mir(later, 3)
            if later // CH > 0:
                sum_wide(later, 0)
    for copy in pending:
        copy.wait_send()


def on_device(nw, nn, trial_x, trial_y, energy, level_shift, resonant_kernel, resonant_list,
              coupling_kernel, coupling_list, partner, exchange_basis):
    rows, vectors = trial_x.shape
    rank = exchange_basis.shape[1]
    blocks, nblk = resonant_list.shape
    patch = rows * nn
    slots = APPS * CH
    bits = nw.bit_length() - 1
    half = vectors // 2
    share = rank // nn
    vmem = pl.BlockSpec(memory_space=pltpu.VMEM)
    smem = pl.BlockSpec(memory_space=pltpu.SMEM)
    anywhere = pl.BlockSpec(memory_space=pl.ANY)
    dma = pltpu.SemaphoreType.DMA
    pieces = [dma((slots, PIECES))] * 14
    flat = (blocks * nblk, BLK, BLK)
    new_x, new_y = pl.pallas_call(
        functools.partial(kernel, nw, nn),
        out_shape=[jax.ShapeDtypeStruct((rows, vectors), F32)] * 2,
        in_specs=[vmem] * 4 + [smem] * 3 + [anywhere] * 3,
        out_specs=[vmem] * 2,
        scratch_shapes=[
            pltpu.VMEM(flat, BF16),
            pltpu.VMEM(flat, BF16),
            pltpu.VMEM((rows, rank), BF16),
            *[pltpu.VMEM((patch // BLK, BLK, vectors), BF16)] * slots,
            pltpu.VMEM((slots, patch // BLK, BLK, vectors), BF16),
            pltpu.VMEM((patch, vectors), F32),
            pltpu.VMEM((64, vectors), F32),
            pltpu.VMEM((patch // BLK, BLK, vectors), BF16),
            pltpu.VMEM((CH, rows, vectors), F32),
            pltpu.VMEM((CH, rows, vectors), F32),
            pltpu.VMEM((slots, nn, half, share), F32),
            pltpu.VMEM((slots, nn - 1, half, share), F32),
            pltpu.VMEM((slots, bits, half, share), F32),
            pltpu.VMEM((slots, bits, half, share), F32),
            pltpu.VMEM((slots, half, share), F32),
            pltpu.VMEM((slots, nn, half, share), BF16),
            dma((3,)),
            *pieces,
            dma((slots, nn - 1)),
            dma((slots, nn - 1)),
            dma((slots, bits)),
            dma((slots, bits)),
            dma((slots, nn - 1)),
            dma((slots, nn - 1)),
        ],
        compiler_params=pltpu.CompilerParams(
            collective_id=0, has_side_effects=True, vmem_limit_bytes=63 * 1024 * 1024
        ),
    )(
        trial_x,
        trial_y,
        energy[:, None],
        level_shift[None, :],
        resonant_list.reshape(-1),
        coupling_list.reshape(-1),
        partner.reshape(-1),
        resonant_kernel.reshape(flat),
        coupling_kernel.reshape(flat),
        exchange_basis,
    )
    return new_x, new_y


def solution(mesh):
    nw, nn = mesh.shape["wide"], mesh.shape["narrow"]
    rows = P(("wide", "narrow"), None)
    return jax.shard_map(
        functools.partial(on_device, nw, nn),
        mesh=mesh,
        in_specs=(
            rows,
            rows,
            P(("wide", "narrow")),
            P(),
            P(("wide", "narrow"), None, None, None),
            rows,
            P(("wide", "narrow"), None, None, None),
            rows,
            P("wide", None),
            rows,
        ),
        out_specs=(rows, rows),
        check_vma=False,
    )
```
